32 devices in a mesh: dp: 8 (over z, core), tensor: 4 (over y, x).
Axes of the slice: x: 2, y: 2, z: 4, core: 2. Of those that a mesh axis runs over, the one named last changes fastest.
Arguments:
- inputs: bfloat16 [2048, 2560], P('dp'), may hold values from -6 to 6
- old_weight: bfloat16 [2560, 2048], P('dp', 'tensor'), may hold values from -0.125 to 0.125
- keep_cols: int32 [1536], replicated, may hold values from 0 to 2047, as said below
- owner: int32 [12], replicated, may hold values from 0 to 3, as said below
- out_grad: bfloat16 [2048, 1536], P('dp', 'tensor'), may hold values from -6 to 6
Outputs:
- projected: bfloat16 [2048, 1536], P('dp', 'tensor')
- gradient_input: bfloat16 [2048, 2560], P('dp', 'tensor')
- weight_grad: float32 [2560, 1536], P('dp', 'tensor')
The draws below stay inside these ranges and needn't reach their ends.
Inputs may be any that keep to these rules, and one draw needn't show every extreme that they name: Each index t of tensor holds old columns [t * 4 * 128, (t + 1) * 4 * 128) and keeps exactly 384 of them, so blocks t * 3 to t * 3 + 2 of keep_cols come from holder t. Every owner receives exactly 3 blocks, and at most 2 blocks from one old holder; some owner receives 2 from one holder.
All inputs are finite; a program needn't handle non-finite values.
Results may differ from the reference program's by a relative error of at most 0.015.
Values may be sent and summed in bfloat16 or wider, within the bound.
A program may use at most 64 MiB of HBM per device.

```python
import jax
import jax.numpy as jnp
from jax import lax

D = 2560
OLD_BLOCKS = 4
NEW_BLOCKS = 3
TOKENS = 2048
FF_OLD = 2048
FF_NEW = 1536
NB = 12
N_TENSOR = 4


def packing_layout(key):
    groups = FF_OLD // (OLD_BLOCKS * 128)
    width_old = OLD_BLOCKS * 128
    blocks = NEW_BLOCKS * groups
    second = jax.random.fold_in(jax.random.fold_in(key, 11), 1)
    third = jax.random.fold_in(jax.random.fold_in(key, 11), 2)
    ranking = jax.vmap(lambda sub: jax.random.permutation(sub, width_old))(jax.random.split(second, groups))
    chosen = ranking < NEW_BLOCKS * 128
    keep = jnp.nonzero(chosen.reshape(-1), size=blocks * 128)[0].astype(jnp.int32)
    sigma = jax.random.permutation(third, groups).astype(jnp.int32)
    index = jnp.arange(blocks, dtype=jnp.int32)
    paired = sigma[jnp.clip(index // 2, 0, groups - 1)]
    single = sigma[jnp.clip(index - 2 * groups, 0, groups - 1)]
    owners = jnp.where(index < 2 * groups, paired, single).astype(jnp.int32)
    return (keep, owners)


def draw_keep_cols(key, part):
    return packing_layout(key)[0]


def draw_owner(key, part):
    return packing_layout(key)[1]


def with_spikes(values, rng, source, target, parts, factor):
    owner, partner = [(jnp.arange(values.shape[position]) // (values.shape[position] // parts)).reshape([-1 if axis == position else 1 for axis in range(values.ndim)]) for position in (source, target)]
    chosen = jax.random.permutation(rng, parts)[partner]
    strong = (owner == chosen) | (owner == (partner + parts // 2) % parts)
    return jnp.where(strong, factor * values, values)


def level_of(own_key, dims, cuts, low, top_value):
    gain = 1.0
    for axis_at, parts in cuts:
        heights = jax.random.uniform(jax.random.fold_in(jax.random.fold_in(own_key, 6), axis_at), (parts,), jnp.float32, low / len(cuts), top_value / len(cuts))
        gain = gain * jnp.repeat(jnp.exp(heights), dims[axis_at] // parts).reshape((-1,) + (1,) * (len(dims) - 1 - axis_at))
    return gain


def centred(stream_key, shape, scale, most, cuts=(), kind=jnp.bfloat16):
    drawn = scale * jax.random.normal(stream_key, shape, jnp.float32)
    if cuts:
        drawn = drawn * level_of(stream_key, shape, cuts, -0.22, 0.18)
    return jnp.clip(drawn, -most, most).astype(kind)


def heavy_noise(rng, shape, deviation, reach, shards, heavy, held_as=jnp.bfloat16):
    array = deviation * jax.random.normal(rng, shape, jnp.float32)
    if shards:
        array = array * level_of(rng, shape, shards, -0.22, 0.18)
    return jnp.clip(with_spikes(array, jax.random.fold_in(rng, 3), *heavy), -reach, reach).astype(held_as)


def setup_inputs(seed: int = 0) -> dict:
    seeds = jax.random.split(jax.random.key(seed), 6)
    return {
        "inputs": heavy_noise(seeds[0], (TOKENS, D), 1.0, 6.0, ((0, 8),), (0, 1, 8, 2.0)),
        "old_weight": centred(seeds[1], (D, FF_OLD), D ** -0.5, 0.125, ((0, 8), (1, 4))),
        "keep_cols": draw_keep_cols(jax.random.fold_in(seeds[5], 71), 0),
        "owner": draw_owner(jax.random.fold_in(seeds[5], 71), 0),
        "out_grad": centred(seeds[4], (TOKENS, FF_NEW), 1.0, 6.0, ((0, 8), (1, 4))),
    }


def reference(inputs, old_weight, keep_cols, owner, out_grad):
    input_rows = inputs.astype(jnp.float32)
    inverse_sigma = lax.rsqrt(lax.optimization_barrier(jnp.mean(input_rows * input_rows, axis=1, keepdims=True)) + 1e-05)
    centered_input = input_rows * inverse_sigma
    normalized_rows = centered_input.astype(jnp.bfloat16)
    order = jnp.argsort(owner, stable=True).astype(jnp.int32)
    columns = keep_cols.reshape(NB, 128)[order].reshape(-1)
    weight = jnp.take(old_weight, columns, axis=1)
    projected = jnp.dot(normalized_rows, weight, preferred_element_type=jnp.float32).astype(jnp.bfloat16)
    share = NEW_BLOCKS * 128
    normalized_gradient = jnp.zeros(input_rows.shape, jnp.float32)
    for group in range(N_TENSOR):
        grad_part = out_grad[:, group * share:(group + 1) * share]
        weight_part = weight[:, group * share:(group + 1) * share]
        partial_term = lax.dot_general(grad_part, weight_part, (((1,), (1,)), ((), ())), preferred_element_type=jnp.float32)
        normalized_gradient = normalized_gradient + partial_term.astype(jnp.bfloat16).astype(jnp.float32)
    inner_product = lax.optimization_barrier(jnp.mean(normalized_gradient * centered_input, axis=1, keepdims=True))
    gradient_input = (inverse_sigma * (normalized_gradient - centered_input * inner_product)).astype(jnp.bfloat16)
    weight_grad = lax.dot_general(normalized_rows, out_grad, (((0,), (0,)), ((), ())), preferred_element_type=jnp.float32)
    return (projected, gradient_input, weight_grad)
```

```python
import functools

import jax
import jax.numpy as jnp
from jax import lax
from jax.experimental import pallas as pl
from jax.experimental.pallas import tpu as pltpu
from jax.sharding import PartitionSpec as P

MESH = pl.DeviceIdType.MESH
BF16 = jnp.bfloat16
F32 = jnp.float32


def fused_kernel(
    groups, ranks, x_ref, old_ref, keep_ref, owner_ref, og_ref,
    proj_ref, gin_ref, wg_ref,
    comp, pack, unpacked, xhat, normed, stripes, acc, dn_send, dn_recv, dot_send, dot_recv,
    sib_send, sib_recv, up_send, up_recv, down_send, down_recv,
    pack_ss, pack_rs, sib_ss, sib_rs, up_ss, up_rs, down_ss, down_rs,
    gup_ss, gdown_ss, gsib_ss, gather_rs, dn_ss, dn_rs, dot_ss, dot_rs,
):
    dp = lax.axis_index("dp")
    ten = lax.axis_index("tensor")
    chips = ranks // 2
    z, core = dp // 2, dp % 2
    rows, width = old_ref.shape
    tokens, features = x_ref.shape
    blocks = owner_ref.shape[0]
    own = blocks // groups
    per = ranks // groups
    share = features // groups
    sibling = z * 2 + (1 - core)

    def peer(k):
        return lax.rem(ten + k, groups)

    def remote(src, dst, ss, rs, **where):
        return pltpu.make_async_remote_copy(
            src_ref=src, dst_ref=dst, send_sem=ss, recv_sem=rs,
            device_id=where, device_id_type=MESH,
        )

    barrier = pltpu.get_barrier_semaphore()
    for k in range(1, groups):
        pl.semaphore_signal(barrier, inc=1, device_id={"tensor": peer(k)}, device_id_type=MESH)
    pl.semaphore_signal(barrier, inc=1, device_id={"dp": sibling}, device_id_type=MESH)

    @pl.when(z > 0)
    def _():
        pl.semaphore_signal(barrier, inc=1, device_id={"dp": dp - 2}, device_id_type=MESH)

    @pl.when(z < chips - 1)
    def _():
        pl.semaphore_signal(barrier, inc=1, device_id={"dp": dp + 2}, device_id_type=MESH)

    column = lax.broadcasted_iota(jnp.int32, (width, 128), 0) + ten * width
    for i in range(own):
        pick = jnp.where(column == keep_ref[pl.ds(ten * own + i, 1), :], 1.0, 0.0).astype(BF16)
        comp[i] = jnp.dot(old_ref[...], pick, preferred_element_type=F32).astype(BF16)
    for k in range(groups):
        target = peer(k)
        first = jnp.int32(own - 1)
        for i in range(own - 2, -1, -1):
            first = jnp.where(owner_ref[ten * own + i] == target, i, first)
        second = jnp.int32(own - 1)
        for i in range(own - 2, 0, -1):
            hit = (owner_ref[ten * own + i] == target) & (i > first)
            second = jnp.where(hit, i, second)
        dst = unpacked if k == 0 else pack
        dst[k, 0] = comp[first]
        dst[k, 1] = comp[second]

    ends = jnp.where(z > 0, 1, 0) + jnp.where(z < chips - 1, 1, 0)
    pl.semaphore_wait(barrier, groups + ends)

    def pack_copy(k):
        return remote(pack.at[k], unpacked.at[k], pack_ss.at[k], pack_rs.at[k], tensor=peer(k))

    for k in range(1, groups):
        pack_copy(k).start()

    total = jnp.zeros((1, tokens), F32)
    for j in range(features // 128):
        part = x_ref[:, j * 128:(j + 1) * 128].astype(F32).T
        xhat[j * 128:(j + 1) * 128, :] = part
        total = total + jnp.sum(part * part, axis=0, keepdims=True)
    inv = lax.rsqrt(total / features + 1e-05)
    for j in range(features // 128):
        part = xhat[j * 128:(j + 1) * 128, :] * inv
        xhat[j * 128:(j + 1) * 128, :] = part
        normed[j * 128:(j + 1) * 128, :] = part.astype(BF16)

    def strip(ref, d):
        return ref[pl.ds(pl.multiple_of(d * rows, 16), rows), :]

    def grad_part(d):
        return jnp.dot(strip(normed, d), og_ref[...], preferred_element_type=F32)

    def sib_copy(c):
        return remote(sib_send.at[c], sib_recv.at[c], sib_ss.at[c], sib_rs.at[c], dp=sibling)

    def up_copy(c):
        return remote(up_send.at[c], up_recv.at[c], up_ss.at[c], up_rs.at[c], dp=dp + 2)

    def down_copy(c):
        return remote(down_send.at[c], down_recv.at[c], down_ss.at[c], down_rs.at[c], dp=dp - 2)

    order = []
    for k in range(chips):
        for c in (chips - 1 - k, k):
            if c not in order:
                order.append(c)
    for c in order:
        sib_send[c] = grad_part(2 * c + 1 - core).astype(BF16)
        sib_copy(c).start()

    def pair_sum(c):
        mine = grad_part(2 * c + core)
        sib_copy(c).wait_recv()
        return mine + sib_recv[c].astype(F32)

    def up_first(c):
        up_send[c] = pair_sum(c).astype(BF16)
        up_copy(c).start()

    def down_first(c):
        down_send[c] = pair_sum(c).astype(BF16)
        down_copy(c).start()

    @pl.when(z == 0)
    def _():
        for c in range(chips - 1, 0, -1):
            up_first(c)

    @pl.when(z == chips - 1)
    def _():
        for c in range(chips - 1):
            down_first(c)

    def chain(k):
        up, down = chips - 1 - k, k

        @pl.when((z > 0) & (z < up))
        def _():
            mine = pair_sum(up)
            up_copy(up).wait_recv()
            up_send[up] = (mine + up_recv[up].astype(F32)).astype(BF16)
            up_copy(up).start()

        @pl.when((z < chips - 1) & (z > down))
        def _():
            mine = pair_sum(down)
            down_copy(down).wait_recv()
            down_send[down] = (mine + down_recv[down].astype(F32)).astype(BF16)
            down_copy(down).start()

    places = [jnp.int32(0) for _ in range(own)]
    count = jnp.int32(0)
    for h in range(groups):
        slot = jnp.int32(0)
        k = lax.rem(ten - h + groups, groups)
        for i in range(own):
            hit = owner_ref[h * own + i] == ten
            for r in range(own):
                places[r] = jnp.where(hit & (count == r), k * 2 + slot, places[r])
            step = jnp.where(hit, 1, 0)
            slot, count = slot + step, count + step
    for k in range(1, groups):
        pack_copy(k).wait_recv()
    for r in range(own):
        stripes[dp, :, r * 128:(r + 1) * 128] = unpacked[places[r] // 2, places[r] % 2]

    def gather_up(d):
        return remote(stripes.at[d], stripes.at[d], gup_ss.at[d], gather_rs.at[d], dp=dp + 2)

    def gather_down(d):
        return remote(stripes.at[d], stripes.at[d], gdown_ss.at[d], gather_rs.at[d], dp=dp - 2)

    def gather_sib(d):
        return remote(stripes.at[d], stripes.at[d], gsib_ss.at[d], gather_rs.at[d], dp=sibling)

    def dn_copy(d):
        k = lax.rem(d // per - ten + groups, groups)
        j = d % per
        return remote(
            dn_send.at[d], dn_recv.at[k, j], dn_ss.at[d], dn_rs.at[k, j], tensor=d // per
        )

    def use(d):
        part = lax.dot_general(
            stripes[d], og_ref[...], (((1,), (1,)), ((), ())), preferred_element_type=F32
        ).astype(BF16)
        dn_send[d] = part

        @pl.when(d // per != ten)
        def _():
            dn_copy(d).start()

        dot_send[...] += jnp.sum(
            (part.astype(F32) * strip(xhat, d)).reshape(rows // 8, 8, tokens), axis=0
        )
        acc[...] += lax.dot_general(
            strip(normed, d), stripes[d], (((0,), (0,)), ((), ())), preferred_element_type=F32
        )

    acc[...] = jnp.zeros_like(acc)
    dot_send[...] = jnp.zeros_like(dot_send)

    @pl.when(z < chips - 1)
    def _():
        gather_up(dp).start()

    @pl.when(z > 0)
    def _():
        gather_down(dp).start()

    gather_sib(dp).start()
    use(dp)

    def from_sibling(chip):
        d = chip * 2 + 1 - core
        gather_sib(d).wait_recv()
        use(d)

    for s in range(1, chips):
        chain(s - 1)

        @pl.when(z - s >= 0)
        def _():
            d = dp - 2 * s
            gather_up(d).wait_recv()

            @pl.when(z < chips - 1)
            def _():
                gather_up(d).start()

            gather_sib(d).start()

        @pl.when(z + s < chips)
        def _():
            d = dp + 2 * s
            gather_down(d).wait_recv()

            @pl.when(z > 0)
            def _():
                gather_down(d).start()

            gather_sib(d).start()

        if s == 1:
            from_sibling(z)

        @pl.when(z - s >= 0)
        def _():
            use(dp - 2 * s)
            from_sibling(z - s)

        @pl.when(z + s < chips)
        def _():
            use(dp + 2 * s)
            from_sibling(z + s)

    def dot_copy(k):
        return remote(dot_send, dot_recv.at[k], dot_ss.at[k], dot_rs.at[k], tensor=peer(k))

    for k in range(1, groups):
        dot_copy(k).start()
    proj_ref[...] = acc[...].astype(BF16)

    sib_total = grad_part(dp)
    sib_copy(z).wait_recv()
    wg_ref[...] = sib_total + sib_recv[z].astype(F32)

    @pl.when(z > 0)
    def _():
        up_copy(z).wait_recv()
        wg_ref[...] += up_recv[z].astype(F32)

    @pl.when(z < chips - 1)
    def _():
        down_copy(z).wait_recv()
        wg_ref[...] += down_recv[z].astype(F32)

    dot = dot_send[...]
    for k in range(1, groups):
        dot_copy(k).wait_recv()
        dot = dot + dot_recv[k]
    mean = jnp.sum(dot, axis=0, keepdims=True) / features
    for j in range(per):
        at = ten * per + j
        full = dn_send[at].astype(F32)
        for k in range(1, groups):
            remote(
                dn_send.at[at], dn_recv.at[k, j], dn_ss.at[at], dn_rs.at[k, j], tensor=peer(k)
            ).wait_recv()
            full = full + dn_recv[k, j].astype(F32)
        acc_t = inv * (full - strip(xhat, at) * mean)
        xhat[pl.ds(pl.multiple_of(at * rows, 16), rows), :] = acc_t
    for j in range(share // 128):
        rows_j = pl.ds(pl.multiple_of(ten * share + j * 128, 128), 128)
        gin_ref[:, j * 128:(j + 1) * 128] = xhat[rows_j, :].T.astype(BF16)

    for k in range(1, groups):
        pack_copy(k).wait_send()
        dot_copy(k).wait_send()
    for c in range(chips):
        sib_copy(c).wait_send()

        @pl.when(c > z)
        def _():
            up_copy(c).wait_send()

        @pl.when(c < z)
        def _():
            down_copy(c).wait_send()

        d = 2 * c + core
        gather_sib(d).wait_send()

        @pl.when((c <= z) & (z < chips - 1))
        def _():
            gather_up(d).wait_send()

        @pl.when((c >= z) & (z > 0))
        def _():
            gather_down(d).wait_send()

    for d in range(ranks):
        @pl.when(d // per != ten)
        def _():
            dn_copy(d).wait_send()


def fused(groups, ranks, inputs, old_weight, keep_cols, owner, out_grad):
    tokens, features = inputs.shape
    rows, _ = old_weight.shape
    cols = out_grad.shape[1]
    own = cols // 128
    chips = ranks // 2
    per = ranks // groups
    stripe = (rows, cols)
    dma = pltpu.SemaphoreType.DMA
    vmem = pl.BlockSpec(memory_space=pltpu.VMEM)
    smem = pl.BlockSpec(memory_space=pltpu.SMEM)
    return pl.pallas_call(
        functools.partial(fused_kernel, groups, ranks),
        out_shape=(
            jax.ShapeDtypeStruct((tokens, cols), BF16),
            jax.ShapeDtypeStruct((tokens, features // groups), BF16),
            jax.ShapeDtypeStruct(stripe, F32),
        ),
        in_specs=[vmem, vmem, vmem, smem, vmem],
        out_specs=(vmem, vmem, vmem),
        scratch_shapes=[
            pltpu.VMEM((own, rows, 128), BF16),
            pltpu.VMEM((groups, 2, rows, 128), BF16),
            pltpu.VMEM((groups, 2, rows, 128), BF16),
            pltpu.VMEM((features, tokens), F32),
            pltpu.VMEM((features, tokens), BF16),
            pltpu.VMEM((ranks,) + stripe, BF16),
            pltpu.VMEM((tokens, cols), F32),
            pltpu.VMEM((ranks, rows, tokens), BF16),
            pltpu.VMEM((groups, per, rows, tokens), BF16),
            pltpu.VMEM((8, tokens), F32),
            pltpu.VMEM((groups, 8, tokens), F32),
        ]
        + [pltpu.VMEM((chips,) + stripe, BF16)] * 6
        + [dma((groups,))] * 2
        + [dma((chips,))] * 6
        + [dma((ranks,))] * 5
        + [dma((groups, per))]
        + [dma((groups,))] * 2,
        compiler_params=pltpu.CompilerParams(
            collective_id=0, has_side_effects=True, vmem_limit_bytes=56 * 1024 * 1024
        ),
    )(inputs, old_weight, keep_cols.reshape(-1, 128), owner, out_grad)


def plain(inputs, old_weight, keep_cols, owner, out_grad):
    groups = lax.axis_size("tensor")
    myself = lax.axis_index("tensor")
    blocks = owner.shape[0]
    own_blocks = blocks // groups
    keep_table = keep_cols.reshape(blocks, 128)
    block_ids = jnp.arange(blocks, dtype=jnp.int32)
    earlier = block_ids[None, :] < block_ids[:, None]
    same_owner = owner[:, None] == owner[None, :]
    owner_rank = jnp.sum(same_owner & earlier, axis=1)
    ranks_here = jnp.arange(own_blocks, dtype=jnp.int32)
    mine_match = (owner[None, :] == myself) & (owner_rank[None, :] == ranks_here[:, None])
    mine_ids = jnp.sum(jnp.where(mine_match, block_ids[None, :], 0), axis=1)
    every_column = lax.all_gather(old_weight, "tensor", axis=1, tiled=True)
    new_stripe = jnp.take(every_column, keep_table[mine_ids].reshape(-1), axis=1)
    expanded_output = inputs.astype(jnp.float32)
    inverse_sigma = lax.rsqrt(
        jnp.mean(expanded_output * expanded_output, axis=1, keepdims=True) + 1e-05
    )
    centered_input = expanded_output * inverse_sigma
    normalized_rows = centered_input.astype(jnp.bfloat16)
    tokens, width = inputs.shape
    piece = lax.all_gather(new_stripe, "dp", axis=0, tiled=True)
    normed_cols = normalized_rows
    proj_sum = jnp.dot(normed_cols, piece, preferred_element_type=jnp.float32)
    partial_term = lax.dot_general(
        out_grad, piece, (((1,), (1,)), ((), ())), preferred_element_type=jnp.float32
    )
    back_sum = partial_term
    proj_sum, back_sum = (proj_sum, back_sum)
    projected = proj_sum.astype(jnp.bfloat16)
    share = width // groups
    reduced_total = lax.psum(back_sum.astype(jnp.bfloat16), "tensor").astype(jnp.float32)
    inner_product = jnp.mean(reduced_total * centered_input, axis=1, keepdims=True)
    complete_gradient = inverse_sigma * (reduced_total - centered_input * inner_product)
    gradient_input = lax.dynamic_slice_in_dim(complete_gradient, myself * share, share, 1).astype(
        jnp.bfloat16
    )
    normed_cols = normalized_rows
    weight_grad = lax.psum_scatter(
        lax.dot_general(
            normed_cols, out_grad, (((0,), (0,)), ((), ())), preferred_element_type=jnp.float32
        ),
        "dp",
        scatter_dimension=0,
        tiled=True,
    )
    return (projected, gradient_input, weight_grad)


def solution(mesh):
    groups, ranks = mesh.shape["tensor"], mesh.shape["dp"]
    placed = (P("dp", None), P("dp", "tensor"), P(), P(), P("dp", "tensor"))

    def local(inputs, old_weight, keep_cols, owner, out_grad):
        rows, share = old_weight.shape[0], inputs.shape[1] // groups
        fits = rows % 16 == 0 and share % 128 == 0 and ranks % groups == 0 and ranks % 2 == 0
        if fits:
            return fused(groups, ranks, inputs, old_weight, keep_cols, owner, out_grad)
        return plain(inputs, old_weight, keep_cols, owner, out_grad)

    return jax.shard_map(
        local,
        mesh=mesh,
        in_specs=placed,
        out_specs=(P("dp", "tensor"), P("dp", "tensor"), P("dp", "tensor")),
        check_vma=False,
    )
```

```python
import functools

import jax
import jax.numpy as jnp
from jax import lax
from jax.experimental import pallas as pl
from jax.experimental.pallas import tpu as pltpu
from jax.sharding import PartitionSpec as P

MESH = pl.DeviceIdType.MESH
BF16 = jnp.bfloat16
F32 = jnp.float32


def fused_kernel(
    groups, ranks, x_ref, old_ref, keep_ref, owner_ref, og_ref,
    proj_ref, gin_ref, wg_ref,
    comp, pack, unpacked, xhat, normed, stripes, acc, dn_send, dn_recv, relay, dot_send, dot_recv,
    sib_send, sib_recv, up_send, up_recv, down_send, down_recv,
    pack_ss, pack_rs, sib_ss, sib_rs, up_ss, up_rs, down_ss, down_rs,
    gup_ss, gdown_ss, gsib_ss, gather_rs, dn_ss, dn_rs, relay_rs, dot_ss, dot_rs,
):
    dp = lax.axis_index("dp")
    ten = lax.axis_index("tensor")
    chips = ranks // 2
    z, core = dp // 2, dp % 2
    rows, width = old_ref.shape
    tokens, features = x_ref.shape
    blocks = owner_ref.shape[0]
    own = blocks // groups
    per = ranks // groups
    share = features // groups
    sibling = z * 2 + (1 - core)

    def peer(k):
        return lax.rem(ten + k, groups)

    def remote(src, dst, ss, rs, **where):
        return pltpu.make_async_remote_copy(
            src_ref=src, dst_ref=dst, send_sem=ss, recv_sem=rs,
            device_id=where, device_id_type=MESH,
        )

    barrier = pltpu.get_barrier_semaphore()
    for k in range(1, groups):
        pl.semaphore_signal(barrier, inc=1, device_id={"tensor": peer(k)}, device_id_type=MESH)
    pl.semaphore_signal(barrier, inc=1, device_id={"dp": sibling}, device_id_type=MESH)

    @pl.when(z > 0)
    def _():
        pl.semaphore_signal(barrier, inc=1, device_id={"dp": dp - 2}, device_id_type=MESH)

    @pl.when(z < chips - 1)
    def _():
        pl.semaphore_signal(barrier, inc=1, device_id={"dp": dp + 2}, device_id_type=MESH)

    column = lax.broadcasted_iota(jnp.int32, (width, 128), 0) + ten * width
    for i in range(own):
        pick = jnp.where(column == keep_ref[pl.ds(ten * own + i, 1), :], 1.0, 0.0).astype(BF16)
        comp[i] = jnp.dot(old_ref[...], pick, preferred_element_type=F32).astype(BF16)
    for k in range(groups):
        target = peer(k)
        first = jnp.int32(own - 1)
        for i in range(own - 2, -1, -1):
            first = jnp.where(owner_ref[ten * own + i] == target, i, first)
        second = jnp.int32(own - 1)
        for i in range(own - 2, 0, -1):
            hit = (owner_ref[ten * own + i] == target) & (i > first)
            second = jnp.where(hit, i, second)
        dst = unpacked if k == 0 else pack
        dst[k, 0] = comp[first]
        dst[k, 1] = comp[second]

    ends = jnp.where(z > 0, 1, 0) + jnp.where(z < chips - 1, 1, 0)
    pl.semaphore_wait(barrier, groups + ends)

    def pack_copy(k):
        return remote(pack.at[k], unpacked.at[k], pack_ss.at[k], pack_rs.at[k], tensor=peer(k))

    for k in range(1, groups):
        pack_copy(k).start()

    total = jnp.zeros((1, tokens), F32)
    for j in range(features // 128):
        part = x_ref[:, j * 128:(j + 1) * 128].astype(F32).T
        xhat[j * 128:(j + 1) * 128, :] = part
        total = total + jnp.sum(part * part, axis=0, keepdims=True)
    inv = lax.rsqrt(total / features + 1e-05)
    for j in range(features // 128):
        part = xhat[j * 128:(j + 1) * 128, :] * inv
        xhat[j * 128:(j + 1) * 128, :] = part
        normed[j * 128:(j + 1) * 128, :] = part.astype(BF16)

    def strip(ref, d):
        return ref[pl.ds(pl.multiple_of(d * rows, 16), rows), :]

    def grad_part(d):
        return jnp.dot(strip(normed, d), og_ref[...], preferred_element_type=F32)

    def sib_copy(c):
        return remote(sib_send.at[c], sib_recv.at[c], sib_ss.at[c], sib_rs.at[c], dp=sibling)

    def up_copy(c):
        return remote(up_send.at[c], up_recv.at[c], up_ss.at[c], up_rs.at[c], dp=dp + 2)

    def down_copy(c):
        return remote(down_send.at[c], down_recv.at[c], down_ss.at[c], down_rs.at[c], dp=dp - 2)

    order = []
    for k in range(chips):
        for c in (chips - 1 - k, k):
            if c not in order:
                order.append(c)
    for c in order:
        sib_send[c] = grad_part(2 * c + 1 - core).astype(BF16)
        sib_copy(c).start()

    def pair_sum(c):
        mine = grad_part(2 * c + core)
        sib_copy(c).wait_recv()
        return mine + sib_recv[c].astype(F32)

    def up_first(c):
        up_send[c] = pair_sum(c).astype(BF16)
        up_copy(c).start()

    def down_first(c):
        down_send[c] = pair_sum(c).astype(BF16)
        down_copy(c).start()

    @pl.when(z == 0)
    def _():
        for c in range(chips - 1, 1, -1):
            up_first(c)

    @pl.when(z == chips - 1)
    def _():
        for c in range(chips - 2):
            down_first(c)

    def chain(k):
        up, down = chips - 1 - k, k

        @pl.when((z > 0) & (z < up))
        def _():
            mine = pair_sum(up)
            up_copy(up).wait_recv()
            up_send[up] = (mine + up_recv[up].astype(F32)).astype(BF16)
            up_copy(up).start()

        @pl.when((z < chips - 1) & (z > down))
        def _():
            mine = pair_sum(down)
            down_copy(down).wait_recv()
            down_send[down] = (mine + down_recv[down].astype(F32)).astype(BF16)
            down_copy(down).start()

    places = [jnp.int32(0) for _ in range(own)]
    count = jnp.int32(0)
    for h in range(groups):
        slot = jnp.int32(0)
        k = lax.rem(ten - h + groups, groups)
        for i in range(own):
            hit = owner_ref[h * own + i] == ten
            for r in range(own):
                places[r] = jnp.where(hit & (count == r), k * 2 + slot, places[r])
            step = jnp.where(hit, 1, 0)
            slot, count = slot + step, count + step
    for k in range(1, groups):
        pack_copy(k).wait_recv()
    for r in range(own):
        stripes[dp, :, r * 128:(r + 1) * 128] = unpacked[places[r] // 2, places[r] % 2]

    def gather_up(d):
        return remote(stripes.at[d], stripes.at[d], gup_ss.at[d], gather_rs.at[d], dp=dp + 2)

    def gather_down(d):
        return remote(stripes.at[d], stripes.at[d], gdown_ss.at[d], gather_rs.at[d], dp=dp - 2)

    def gather_sib(d):
        return remote(stripes.at[d], stripes.at[d], gsib_ss.at[d], gather_rs.at[d], dp=sibling)

    half = rows // 2

    def flip(bit):
        x, y = ten % 2, ten // 2
        return y * 2 + (1 - x) if bit == 1 else (1 - y) * 2 + x

    def rows_of(h):
        return pl.ds(h * half, half)

    def dn_copy(d, bit, h):
        j = d % per
        return remote(
            dn_send.at[d, rows_of(h)], dn_recv.at[bit - 1, j, rows_of(h)],
            dn_ss.at[d, h], dn_rs.at[bit - 1, j, h], tensor=flip(bit),
        )

    def relay_copy(d, bit):
        h = bit - 1
        return remote(
            dn_send.at[d, rows_of(h)], relay.at[d], dn_ss.at[d, h], relay_rs.at[d],
            tensor=flip(bit),
        )

    def is_near(d, bit):
        return d // per == flip(bit)

    def is_far(d):
        return (d // per != ten) & (d // per != flip(1)) & (d // per != flip(2))

    def use(d):
        part = lax.dot_general(
            stripes[d], og_ref[...], (((1,), (1,)), ((), ())), preferred_element_type=F32
        ).astype(BF16)
        dn_send[d] = part

        @pl.when(is_far(d))
        def _():
            relay_copy(d, 1).start()
            relay_copy(d, 2).start()

        for bit in (1, 2):
            @pl.when(is_near(d, bit))
            def _():
                dn_copy(d, bit, bit - 1).start()

        dot_send[...] += jnp.sum(
            (part.astype(F32) * strip(xhat, d)).reshape(rows // 8, 8, tokens), axis=0
        )
        acc[...] += lax.dot_general(
            strip(normed, d), stripes[d], (((0,), (0,)), ((), ())), preferred_element_type=F32
        )

    def pass_on(d):
        for bit in (1, 2):
            @pl.when(is_near(d, bit))
            def _():
                h = 2 - bit
                relay_copy(d, 3 - bit).wait_recv()
                mine = dn_send[d, rows_of(h)].astype(F32)
                dn_send[d, rows_of(h)] = (mine + relay[d].astype(F32)).astype(BF16)
                dn_copy(d, bit, h).start()

    def pass_on_pair(s):
        @pl.when(z - s >= 0)
        def _():
            pass_on(dp - 2 * s)
            pass_on((z - s) * 2 + 1 - core)

        if s > 0:
            @pl.when(z + s < chips)
            def _():
                pass_on(dp + 2 * s)
                pass_on((z + s) * 2 + 1 - core)

    acc[...] = jnp.zeros_like(acc)
    dot_send[...] = jnp.zeros_like(dot_send)

    @pl.when(z < chips - 1)
    def _():
        gather_up(dp).start()

    @pl.when(z > 0)
    def _():
        gather_down(dp).start()

    gather_sib(dp).start()
    use(dp)

    def from_sibling(chip):
        d = chip * 2 + 1 - core
        gather_sib(d).wait_recv()
        use(d)

    from_sibling(z)
    for s in range(1, chips):
        chain(s - 1)

        @pl.when(z - s >= 0)
        def _():
            d = dp - 2 * s
            gather_up(d).wait_recv()

            @pl.when(z < chips - 1)
            def _():
                gather_up(d).start()

            gather_sib(d).start()

        @pl.when(z + s < chips)
        def _():
            d = dp + 2 * s
            gather_down(d).wait_recv()

            @pl.when(z > 0)
            def _():
                gather_down(d).start()

            gather_sib(d).start()

        if s == 1:
            @pl.when(z == 0)
            def _():
                up_first(1)

            @pl.when(z == chips - 1)
            def _():
                down_first(chips - 2)

        pass_on_pair(s - 1)

        @pl.when(z - s >= 0)
        def _():
            use(dp - 2 * s)
            from_sibling(z - s)

        @pl.when(z + s < chips)
        def _():
            use(dp + 2 * s)
            from_sibling(z + s)

    def dot_copy(k):
        return remote(dot_send, dot_recv.at[k], dot_ss.at[k], dot_rs.at[k], tensor=peer(k))

    for k in range(1, groups):
        dot_copy(k).start()
    pass_on_pair(chips - 1)
    proj_ref[...] = acc[...].astype(BF16)

    sib_total = grad_part(dp)
    sib_copy(z).wait_recv()
    wg_ref[...] = sib_total + sib_recv[z].astype(F32)

    @pl.when(z > 0)
    def _():
        up_copy(z).wait_recv()
        wg_ref[...] += up_recv[z].astype(F32)

    @pl.when(z < chips - 1)
    def _():
        down_copy(z).wait_recv()
        wg_ref[...] += down_recv[z].astype(F32)

    dot = dot_send[...]
    for k in range(1, groups):
        dot_copy(k).wait_recv()
        dot = dot + dot_recv[k]
    mean = jnp.sum(dot, axis=0, keepdims=True) / features
    for j in range(per):
        at = ten * per + j
        full = dn_send[at].astype(F32)
        for bit in (1, 2):
            for h in (0, 1):
                dn_copy(at, bit, h).wait_recv()
            full = full + dn_recv[bit - 1, j].astype(F32)
        acc_t = inv * (full - strip(xhat, at) * mean)
        xhat[pl.ds(pl.multiple_of(at * rows, 16), rows), :] = acc_t
    for j in range(share // 128):
        rows_j = pl.ds(pl.multiple_of(ten * share + j * 128, 128), 128)
        gin_ref[:, j * 128:(j + 1) * 128] = xhat[rows_j, :].T.astype(BF16)

    for k in range(1, groups):
        pack_copy(k).wait_send()
        dot_copy(k).wait_send()
    for c in range(chips):
        sib_copy(c).wait_send()

        @pl.when(c > z)
        def _():
            up_copy(c).wait_send()

        @pl.when(c < z)
        def _():
            down_copy(c).wait_send()

        d = 2 * c + core
        gather_sib(d).wait_send()

        @pl.when((c <= z) & (z < chips - 1))
        def _():
            gather_up(d).wait_send()

        @pl.when((c >= z) & (z > 0))
        def _():
            gather_down(d).wait_send()

    for d in range(ranks):
        @pl.when(d // per != ten)
        def _():
            for h in (0, 1):
                dn_copy(d, 1, h).wait_send()


def fused(groups, ranks, inputs, old_weight, keep_cols, owner, out_grad):
    tokens, features = inputs.shape
    rows, _ = old_weight.shape
    cols = out_grad.shape[1]
    own = cols // 128
    chips = ranks // 2
    per = ranks // groups
    stripe = (rows, cols)
    dma = pltpu.SemaphoreType.DMA
    vmem = pl.BlockSpec(memory_space=pltpu.VMEM)
    smem = pl.BlockSpec(memory_space=pltpu.SMEM)
    return pl.pallas_call(
        functools.partial(fused_kernel, groups, ranks),
        out_shape=(
            jax.ShapeDtypeStruct((tokens, cols), BF16),
            jax.ShapeDtypeStruct((tokens, features // groups), BF16),
            jax.ShapeDtypeStruct(stripe, F32),
        ),
        in_specs=[vmem, vmem, vmem, smem, vmem],
        out_specs=(vmem, vmem, vmem),
        scratch_shapes=[
            pltpu.VMEM((own, rows, 128), BF16),
            pltpu.VMEM((groups, 2, rows, 128), BF16),
            pltpu.VMEM((groups, 2, rows, 128), BF16),
            pltpu.VMEM((features, tokens), F32),
            pltpu.VMEM((features, tokens), BF16),
            pltpu.VMEM((ranks,) + stripe, BF16),
            pltpu.VMEM((tokens, cols), F32),
            pltpu.VMEM((ranks, rows, tokens), BF16),
            pltpu.VMEM((2, per, rows, tokens), BF16),
            pltpu.VMEM((ranks, rows // 2, tokens), BF16),
            pltpu.VMEM((8, tokens), F32),
            pltpu.VMEM((groups, 8, tokens), F32),
        ]
        + [pltpu.VMEM((chips,) + stripe, BF16)] * 6
        + [dma((groups,))] * 2
        + [dma((chips,))] * 6
        + [dma((ranks,))] * 4
        + [dma((ranks, 2)), dma((2, per, 2)), dma((ranks,))]
        + [dma((groups,))] * 2,
        compiler_params=pltpu.CompilerParams(
            collective_id=0, has_side_effects=True, vmem_limit_bytes=26 * 1024 * 1024
        ),
    )(inputs, old_weight, keep_cols.reshape(-1, 128), owner, out_grad)


def plain(inputs, old_weight, keep_cols, owner, out_grad):
    groups = lax.axis_size("tensor")
    myself = lax.axis_index("tensor")
    blocks = owner.shape[0]
    own_blocks = blocks // groups
    keep_table = keep_cols.reshape(blocks, 128)
    block_ids = jnp.arange(blocks, dtype=jnp.int32)
    earlier = block_ids[None, :] < block_ids[:, None]
    same_owner = owner[:, None] == owner[None, :]
    owner_rank = jnp.sum(same_owner & earlier, axis=1)
    ranks_here = jnp.arange(own_blocks, dtype=jnp.int32)
    mine_match = (owner[None, :] == myself) & (owner_rank[None, :] == ranks_here[:, None])
    mine_ids = jnp.sum(jnp.where(mine_match, block_ids[None, :], 0), axis=1)
    every_column = lax.all_gather(old_weight, "tensor", axis=1, tiled=True)
    new_stripe = jnp.take(every_column, keep_table[mine_ids].reshape(-1), axis=1)
    expanded_output = inputs.astype(jnp.float32)
    inverse_sigma = lax.rsqrt(
        jnp.mean(expanded_output * expanded_output, axis=1, keepdims=True) + 1e-05
    )
    centered_input = expanded_output * inverse_sigma
    normalized_rows = centered_input.astype(jnp.bfloat16)
    tokens, width = inputs.shape
    piece = lax.all_gather(new_stripe, "dp", axis=0, tiled=True)
    normed_cols = normalized_rows
    proj_sum = jnp.dot(normed_cols, piece, preferred_element_type=jnp.float32)
    partial_term = lax.dot_general(
        out_grad, piece, (((1,), (1,)), ((), ())), preferred_element_type=jnp.float32
    )
    back_sum = partial_term
    proj_sum, back_sum = (proj_sum, back_sum)
    projected = proj_sum.astype(jnp.bfloat16)
    share = width // groups
    reduced_total = lax.psum(back_sum.astype(jnp.bfloat16), "tensor").astype(jnp.float32)
    inner_product = jnp.mean(reduced_total * centered_input, axis=1, keepdims=True)
    complete_gradient = inverse_sigma * (reduced_total - centered_input * inner_product)
    gradient_input = lax.dynamic_slice_in_dim(complete_gradient, myself * share, share, 1).astype(
        jnp.bfloat16
    )
    normed_cols = normalized_rows
    weight_grad = lax.psum_scatter(
        lax.dot_general(
            normed_cols, out_grad, (((0,), (0,)), ((), ())), preferred_element_type=jnp.float32
        ),
        "dp",
        scatter_dimension=0,
        tiled=True,
    )
    return (projected, gradient_input, weight_grad)


def solution(mesh):
    groups, ranks = mesh.shape["tensor"], mesh.shape["dp"]
    placed = (P("dp", None), P("dp", "tensor"), P(), P(), P("dp", "tensor"))

    def local(inputs, old_weight, keep_cols, owner, out_grad):
        rows, share = old_weight.shape[0], inputs.shape[1] // groups
        fits = rows % 32 == 0 and share % 128 == 0 and groups == 4 and ranks % 4 == 0
        if fits:
            return fused(groups, ranks, inputs, old_weight, keep_cols, owner, out_grad)
        return plain(inputs, old_weight, keep_cols, owner, out_grad)

    return jax.shard_map(
        local,
        mesh=mesh,
        in_specs=placed,
        out_specs=(P("dp", "tensor"), P("dp", "tensor"), P("dp", "tensor")),
        check_vma=False,
    )
```

```python
import functools

import jax
import jax.numpy as jnp
from jax import lax
from jax.experimental import pallas as pl
from jax.experimental.pallas import tpu as pltpu
from jax.sharding import PartitionSpec as P

MESH = pl.DeviceIdType.MESH
BF16 = jnp.bfloat16
F32 = jnp.float32


def fused_kernel(
    groups, ranks, x_ref, old_ref, keep_ref, owner_ref, og_ref,
    proj_ref, gin_ref, wg_ref,
    comp, pack, unpacked, xhat, normed, stripes, acc, dn_send, dn_recv, relay, dot_send, dot_recv,
    sib_send, sib_recv, up_send, up_recv, down_send, down_recv,
    pack_ss, pack_rs, sib_ss, sib_rs, up_ss, up_rs, down_ss, down_rs,
    gup_ss, gdown_ss, gsib_ss, gather_rs, dn_ss, dn_rs, relay_rs, dot_ss, dot_rs,
):
    dp = lax.axis_index("dp")
    ten = lax.axis_index("tensor")
    chips = ranks // 2
    z, core = dp // 2, dp % 2
    rows, width = old_ref.shape
    tokens, features = x_ref.shape
    blocks = owner_ref.shape[0]
    own = blocks // groups
    per = ranks // groups
    share = features // groups
    sibling = z * 2 + (1 - core)

    def peer(k):
        return lax.rem(ten + k, groups)

    def remote(src, dst, ss, rs, **where):
        return pltpu.make_async_remote_copy(
            src_ref=src, dst_ref=dst, send_sem=ss, recv_sem=rs,
            device_id=where, device_id_type=MESH,
        )

    barrier = pltpu.get_barrier_semaphore()
    for k in range(1, groups):
        pl.semaphore_signal(barrier, inc=1, device_id={"tensor": peer(k)}, device_id_type=MESH)
    pl.semaphore_signal(barrier, inc=1, device_id={"dp": sibling}, device_id_type=MESH)

    @pl.when(z > 0)
    def _():
        pl.semaphore_signal(barrier, inc=1, device_id={"dp": dp - 2}, device_id_type=MESH)

    @pl.when(z < chips - 1)
    def _():
        pl.semaphore_signal(barrier, inc=1, device_id={"dp": dp + 2}, device_id_type=MESH)

    column = lax.broadcasted_iota(jnp.int32, (width, 128), 0) + ten * width
    for i in range(own):
        pick = jnp.where(column == keep_ref[pl.ds(ten * own + i, 1), :], 1.0, 0.0).astype(BF16)
        comp[i] = jnp.dot(old_ref[...], pick, preferred_element_type=F32).astype(BF16)
    for k in range(groups):
        target = peer(k)
        first = jnp.int32(own - 1)
        for i in range(own - 2, -1, -1):
            first = jnp.where(owner_ref[ten * own + i] == target, i, first)
        second = jnp.int32(own - 1)
        for i in range(own - 2, 0, -1):
            hit = (owner_ref[ten * own + i] == target) & (i > first)
            second = jnp.where(hit, i, second)
        dst = unpacked if k == 0 else pack
        dst[k, 0] = comp[first]
        dst[k, 1] = comp[second]

    ends = jnp.where(z > 0, 1, 0) + jnp.where(z < chips - 1, 1, 0)
    pl.semaphore_wait(barrier, groups + ends)

    def pack_copy(k):
        return remote(pack.at[k], unpacked.at[k], pack_ss.at[k], pack_rs.at[k], tensor=peer(k))

    for k in range(1, groups):
        pack_copy(k).start()

    total = jnp.zeros((1, tokens), F32)
    for j in range(features // 128):
        part = x_ref[:, j * 128:(j + 1) * 128].astype(F32).T
        xhat[j * 128:(j + 1) * 128, :] = part
        total = total + jnp.sum(part * part, axis=0, keepdims=True)
    inv = lax.rsqrt(total / features + 1e-05)
    for j in range(features // 128):
        part = xhat[j * 128:(j + 1) * 128, :] * inv
        xhat[j * 128:(j + 1) * 128, :] = part
        normed[j * 128:(j + 1) * 128, :] = part.astype(BF16)

    def strip(ref, d):
        return ref[pl.ds(pl.multiple_of(d * rows, 16), rows), :]

    def grad_part(d):
        return jnp.dot(strip(normed, d), og_ref[...], preferred_element_type=F32)

    def sib_copy(c):
        return remote(sib_send.at[c], sib_recv.at[c], sib_ss.at[c], sib_rs.at[c], dp=sibling)

    def up_copy(c):
        return remote(up_send.at[c], up_recv.at[c], up_ss.at[c], up_rs.at[c], dp=dp + 2)

    def down_copy(c):
        return remote(down_send.at[c], down_recv.at[c], down_ss.at[c], down_rs.at[c], dp=dp - 2)

    order = []
    for k in range(chips):
        for c in (chips - 1 - k, k):
            if c not in order:
                order.append(c)
    for c in order:
        sib_send[c] = grad_part(2 * c + 1 - core).astype(BF16)
        sib_copy(c).start()

    def pair_sum(c):
        mine = grad_part(2 * c + core)
        sib_copy(c).wait_recv()
        return mine + sib_recv[c].astype(F32)

    def up_first(c):
        up_send[c] = pair_sum(c).astype(BF16)
        up_copy(c).start()

    def down_first(c):
        down_send[c] = pair_sum(c).astype(BF16)
        down_copy(c).start()

    @pl.when(z == 0)
    def _():
        for c in range(chips - 1, 1, -1):
            up_first(c)
            if c > 2:
                up_copy(c).wait_send()

    @pl.when(z == chips - 1)
    def _():
        for c in range(chips - 2):
            down_first(c)
            if c < chips - 3:
                down_copy(c).wait_send()

    def chain_up(up):
        mine = pair_sum(up)
        up_copy(up).wait_recv()
        up_send[up] = (mine + up_recv[up].astype(F32)).astype(BF16)
        up_copy(up).start()

    def chain_down(down):
        mine = pair_sum(down)
        down_copy(down).wait_recv()
        down_send[down] = (mine + down_recv[down].astype(F32)).astype(BF16)
        down_copy(down).start()

    @pl.when((z == 1) & (z < chips - 1))
    def _():
        chain_up(chips - 1)

    @pl.when((z == chips - 2) & (z > 0))
    def _():
        chain_down(0)

    def chain(k):
        up, down = chips - 1 - k, k

        @pl.when((z > (1 if k == 0 else 0)) & (z < up))
        def _():
            chain_up(up)

        @pl.when((z < chips - (2 if k == 0 else 1)) & (z > down))
        def _():
            chain_down(down)

    places = [jnp.int32(0) for _ in range(own)]
    count = jnp.int32(0)
    for h in range(groups):
        slot = jnp.int32(0)
        k = lax.rem(ten - h + groups, groups)
        for i in range(own):
            hit = owner_ref[h * own + i] == ten
            for r in range(own):
                places[r] = jnp.where(hit & (count == r), k * 2 + slot, places[r])
            step = jnp.where(hit, 1, 0)
            slot, count = slot + step, count + step
    for k in range(1, groups):
        pack_copy(k).wait_recv()
    for r in range(own):
        stripes[dp, :, r * 128:(r + 1) * 128] = unpacked[places[r] // 2, places[r] % 2]

    def gather_up(d):
        return remote(stripes.at[d], stripes.at[d], gup_ss.at[d], gather_rs.at[d], dp=dp + 2)

    def gather_down(d):
        return remote(stripes.at[d], stripes.at[d], gdown_ss.at[d], gather_rs.at[d], dp=dp - 2)

    def gather_sib(d):
        return remote(stripes.at[d], stripes.at[d], gsib_ss.at[d], gather_rs.at[d], dp=sibling)

    half = rows // 2

    def flip(bit):
        x, y = ten % 2, ten // 2
        return y * 2 + (1 - x) if bit == 1 else (1 - y) * 2 + x

    def rows_of(h):
        return pl.ds(h * half, half)

    def dn_copy(d, bit, h):
        j = d % per
        return remote(
            dn_send.at[d, rows_of(h)], dn_recv.at[bit - 1, j, rows_of(h)],
            dn_ss.at[d, h], dn_rs.at[bit - 1, j, h], tensor=flip(bit),
        )

    def relay_copy(d, bit):
        h = bit - 1
        return remote(
            dn_send.at[d, rows_of(h)], relay.at[d], dn_ss.at[d, h], relay_rs.at[d],
            tensor=flip(bit),
        )

    def is_near(d, bit):
        return d // per == flip(bit)

    def is_far(d):
        return (d // per != ten) & (d // per != flip(1)) & (d // per != flip(2))

    def use(d):
        part = lax.dot_general(
            stripes[d], og_ref[...], (((1,), (1,)), ((), ())), preferred_element_type=F32
        ).astype(BF16)
        dn_send[d] = part

        @pl.when(is_far(d))
        def _():
            relay_copy(d, 1).start()
            relay_copy(d, 2).start()

        for bit in (1, 2):
            @pl.when(is_near(d, bit))
            def _():
                dn_copy(d, bit, bit - 1).start()

        dot_send[...] += jnp.sum(
            (part.astype(F32) * strip(xhat, d)).reshape(rows // 8, 8, tokens), axis=0
        )
        acc[...] += lax.dot_general(
            strip(normed, d), stripes[d], (((0,), (0,)), ((), ())), preferred_element_type=F32
        )

    def pass_on(d):
        for bit in (1, 2):
            @pl.when(is_near(d, bit))
            def _():
                h = 2 - bit
                relay_copy(d, 3 - bit).wait_recv()
                mine = dn_send[d, rows_of(h)].astype(F32)
                dn_send[d, rows_of(h)] = (mine + relay[d].astype(F32)).astype(BF16)
                dn_copy(d, bit, h).start()

    def pass_on_pair(s):
        @pl.when(z - s >= 0)
        def _():
            pass_on(dp - 2 * s)
            pass_on((z - s) * 2 + 1 - core)

        if s > 0:
            @pl.when(z + s < chips)
            def _():
                pass_on(dp + 2 * s)
                pass_on((z + s) * 2 + 1 - core)

    acc[...] = jnp.zeros_like(acc)
    dot_send[...] = jnp.zeros_like(dot_send)

    @pl.when(z < chips - 1)
    def _():
        gather_up(dp).start()

    @pl.when(z > 0)
    def _():
        gather_down(dp).start()

    gather_sib(dp).start()
    use(dp)

    def from_sibling(chip):
        d = chip * 2 + 1 - core
        gather_sib(d).wait_recv()
        use(d)

    from_sibling(z)
    for s in range(1, chips):
        @pl.when(z - s >= 0)
        def _():
            d = dp - 2 * s
            gather_up(d).wait_recv()

            @pl.when(z < chips - 1)
            def _():
                gather_up(d).start()

            gather_sib(d).start()

        @pl.when(z + s < chips)
        def _():
            d = dp + 2 * s
            gather_down(d).wait_recv()

            @pl.when(z > 0)
            def _():
                gather_down(d).start()

            gather_sib(d).start()

        if s == 1:
            @pl.when(z == 0)
            def _():
                up_first(1)

            @pl.when(z == chips - 1)
            def _():
                down_first(chips - 2)

        pass_on_pair(s - 1)

        if s == max(chips - 2, 1):
            for k in range(chips - 1):
                chain(k)

        @pl.when(z - s >= 0)
        def _():
            use(dp - 2 * s)
            from_sibling(z - s)

        @pl.when(z + s < chips)
        def _():
            use(dp + 2 * s)
            from_sibling(z + s)

    def dot_copy(k):
        return remote(dot_send, dot_recv.at[k], dot_ss.at[k], dot_rs.at[k], tensor=peer(k))

    for k in range(1, groups):
        dot_copy(k).start()
    pass_on_pair(chips - 1)
    proj_ref[...] = acc[...].astype(BF16)

    sib_total = grad_part(dp)
    sib_copy(z).wait_recv()
    wg_ref[...] = sib_total + sib_recv[z].astype(F32)

    @pl.when(z > 0)
    def _():
        up_copy(z).wait_recv()
        wg_ref[...] += up_recv[z].astype(F32)

    @pl.when(z < chips - 1)
    def _():
        down_copy(z).wait_recv()
        wg_ref[...] += down_recv[z].astype(F32)

    dot = dot_send[...]
    for k in range(1, groups):
        dot_copy(k).wait_recv()
        dot = dot + dot_recv[k]
    mean = jnp.sum(dot, axis=0, keepdims=True) / features
    for j in range(per):
        at = ten * per + j
        full = dn_send[at].astype(F32)
        for bit in (1, 2):
            for h in (0, 1):
                dn_copy(at, bit, h).wait_recv()
            full = full + dn_recv[bit - 1, j].astype(F32)
        acc_t = inv * (full - strip(xhat, at) * mean)
        xhat[pl.ds(pl.multiple_of(at * rows, 16), rows), :] = acc_t
    for j in range(share // 128):
        rows_j = pl.ds(pl.multiple_of(ten * share + j * 128, 128), 128)
        gin_ref[:, j * 128:(j + 1) * 128] = xhat[rows_j, :].T.astype(BF16)

    for k in range(1, groups):
        pack_copy(k).wait_send()
        dot_copy(k).wait_send()
    for c in range(chips):
        sib_copy(c).wait_send()

        @pl.when((c > z) & ((z > 0) | (c <= 2)))
        def _():
            up_copy(c).wait_send()

        @pl.when((c < z) & ((z < chips - 1) | (c >= chips - 3)))
        def _():
            down_copy(c).wait_send()

        d = 2 * c + core
        gather_sib(d).wait_send()

        @pl.when((c <= z) & (z < chips - 1))
        def _():
            gather_up(d).wait_send()

        @pl.when((c >= z) & (z > 0))
        def _():
            gather_down(d).wait_send()

    for d in range(ranks):
        @pl.when(d // per != ten)
        def _():
            for h in (0, 1):
                dn_copy(d, 1, h).wait_send()


def fused(groups, ranks, inputs, old_weight, keep_cols, owner, out_grad):
    tokens, features = inputs.shape
    rows, _ = old_weight.shape
    cols = out_grad.shape[1]
    own = cols // 128
    chips = ranks // 2
    per = ranks // groups
    stripe = (rows, cols)
    dma = pltpu.SemaphoreType.DMA
    vmem = pl.BlockSpec(memory_space=pltpu.VMEM)
    smem = pl.BlockSpec(memory_space=pltpu.SMEM)
    return pl.pallas_call(
        functools.partial(fused_kernel, groups, ranks),
        out_shape=(
            jax.ShapeDtypeStruct((tokens, cols), BF16),
            jax.ShapeDtypeStruct((tokens, features // groups), BF16),
            jax.ShapeDtypeStruct(stripe, F32),
        ),
        in_specs=[vmem, vmem, vmem, smem, vmem],
        out_specs=(vmem, vmem, vmem),
        scratch_shapes=[
            pltpu.VMEM((own, rows, 128), BF16),
            pltpu.VMEM((groups, 2, rows, 128), BF16),
            pltpu.VMEM((groups, 2, rows, 128), BF16),
            pltpu.VMEM((features, tokens), F32),
            pltpu.VMEM((features, tokens), BF16),
            pltpu.VMEM((ranks,) + stripe, BF16),
            pltpu.VMEM((tokens, cols), F32),
            pltpu.VMEM((ranks, rows, tokens), BF16),
            pltpu.VMEM((2, per, rows, tokens), BF16),
            pltpu.VMEM((ranks, rows // 2, tokens), BF16),
            pltpu.VMEM((8, tokens), F32),
            pltpu.VMEM((groups, 8, tokens), F32),
        ]
        + [pltpu.VMEM((chips,) + stripe, BF16)] * 6
        + [dma((groups,))] * 2
        + [dma((chips,))] * 6
        + [dma((ranks,))] * 4
        + [dma((ranks, 2)), dma((2, per, 2)), dma((ranks,))]
        + [dma((groups,))] * 2,
        compiler_params=pltpu.CompilerParams(
            collective_id=0, has_side_effects=True, vmem_limit_bytes=26 * 1024 * 1024
        ),
    )(inputs, old_weight, keep_cols.reshape(-1, 128), owner, out_grad)


def plain(inputs, old_weight, keep_cols, owner, out_grad):
    groups = lax.axis_size("tensor")
    myself = lax.axis_index("tensor")
    blocks = owner.shape[0]
    own_blocks = blocks // groups
    keep_table = keep_cols.reshape(blocks, 128)
    block_ids = jnp.arange(blocks, dtype=jnp.int32)
    earlier = block_ids[None, :] < block_ids[:, None]
    same_owner = owner[:, None] == owner[None, :]
    owner_rank = jnp.sum(same_owner & earlier, axis=1)
    ranks_here = jnp.arange(own_blocks, dtype=jnp.int32)
    mine_match = (owner[None, :] == myself) & (owner_rank[None, :] == ranks_here[:, None])
    mine_ids = jnp.sum(jnp.where(mine_match, block_ids[None, :], 0), axis=1)
    every_column = lax.all_gather(old_weight, "tensor", axis=1, tiled=True)
    new_stripe = jnp.take(every_column, keep_table[mine_ids].reshape(-1), axis=1)
    expanded_output = inputs.astype(jnp.float32)
    inverse_sigma = lax.rsqrt(
        jnp.mean(expanded_output * expanded_output, axis=1, keepdims=True) + 1e-05
    )
    centered_input = expanded_output * inverse_sigma
    normalized_rows = centered_input.astype(jnp.bfloat16)
    tokens, width = inputs.shape
    piece = lax.all_gather(new_stripe, "dp", axis=0, tiled=True)
    normed_cols = normalized_rows
    proj_sum = jnp.dot(normed_cols, piece, preferred_element_type=jnp.float32)
    partial_term = lax.dot_general(
        out_grad, piece, (((1,), (1,)), ((), ())), preferred_element_type=jnp.float32
    )
    back_sum = partial_term
    proj_sum, back_sum = (proj_sum, back_sum)
    projected = proj_sum.astype(jnp.bfloat16)
    share = width // groups
    reduced_total = lax.psum(back_sum.astype(jnp.bfloat16), "tensor").astype(jnp.float32)
    inner_product = jnp.mean(reduced_total * centered_input, axis=1, keepdims=True)
    complete_gradient = inverse_sigma * (reduced_total - centered_input * inner_product)
    gradient_input = lax.dynamic_slice_in_dim(complete_gradient, myself * share, share, 1).astype(
        jnp.bfloat16
    )
    normed_cols = normalized_rows
    weight_grad = lax.psum_scatter(
        lax.dot_general(
            normed_cols, out_grad, (((0,), (0,)), ((), ())), preferred_element_type=jnp.float32
        ),
        "dp",
        scatter_dimension=0,
        tiled=True,
    )
    return (projected, gradient_input, weight_grad)


def solution(mesh):
    groups, ranks = mesh.shape["tensor"], mesh.shape["dp"]
    placed = (P("dp", None), P("dp", "tensor"), P(), P(), P("dp", "tensor"))

    def local(inputs, old_weight, keep_cols, owner, out_grad):
        rows, share = old_weight.shape[0], inputs.shape[1] // groups
        fits = rows % 32 == 0 and share % 128 == 0 and groups == 4 and ranks % 4 == 0
        if fits:
            return fused(groups, ranks, inputs, old_weight, keep_cols, owner, out_grad)
        return plain(inputs, old_weight, keep_cols, owner, out_grad)

    return jax.shard_map(
        local,
        mesh=mesh,
        in_specs=placed,
        out_specs=(P("dp", "tensor"), P("dp", "tensor"), P("dp", "tensor")),
        check_vma=False,
    )
```

```python
import functools

import jax
import jax.numpy as jnp
from jax import lax
from jax.experimental import pallas as pl
from jax.experimental.pallas import tpu as pltpu
from jax.sharding import PartitionSpec as P

MESH = pl.DeviceIdType.MESH
BF16 = jnp.bfloat16
F32 = jnp.float32


def fused_kernel(
    groups, ranks, x_ref, old_ref, keep_ref, owner_ref, og_ref,
    proj_ref, gin_ref, wg_ref,
    comp, pack, unpacked, xhat, normed, stripes, acc, dn_send, dn_recv, relay, dot_send, dot_recv,
    sib_send, sib_recv, up_send, up_recv, down_send, down_recv,
    pack_ss, pack_rs, sib_ss, sib_rs, up_ss, up_rs, down_ss, down_rs,
    gup_ss, gdown_ss, gsib_ss, gather_rs, dn_ss, dn_rs, relay_rs, dot_ss, dot_rs,
):
    dp = lax.axis_index("dp")
    ten = lax.axis_index("tensor")
    chips = ranks // 2
    z, core = dp // 2, dp % 2
    rows, width = old_ref.shape
    tokens, features = x_ref.shape
    blocks = owner_ref.shape[0]
    own = blocks // groups
    per = ranks // groups
    share = features // groups
    sibling = z * 2 + (1 - core)

    def peer(k):
        return lax.rem(ten + k, groups)

    def remote(src, dst, ss, rs, **where):
        return pltpu.make_async_remote_copy(
            src_ref=src, dst_ref=dst, send_sem=ss, recv_sem=rs,
            device_id=where, device_id_type=MESH,
        )

    barrier = pltpu.get_barrier_semaphore()
    for k in range(1, groups):
        pl.semaphore_signal(barrier, inc=1, device_id={"tensor": peer(k)}, device_id_type=MESH)
    pl.semaphore_signal(barrier, inc=1, device_id={"dp": sibling}, device_id_type=MESH)

    @pl.when(z > 0)
    def _():
        pl.semaphore_signal(barrier, inc=1, device_id={"dp": dp - 2}, device_id_type=MESH)

    @pl.when(z < chips - 1)
    def _():
        pl.semaphore_signal(barrier, inc=1, device_id={"dp": dp + 2}, device_id_type=MESH)

    column = lax.broadcasted_iota(jnp.int32, (width, 128), 0) + ten * width
    for i in range(own):
        pick = jnp.where(column == keep_ref[pl.ds(ten * own + i, 1), :], 1.0, 0.0).astype(BF16)
        comp[i] = jnp.dot(old_ref[...], pick, preferred_element_type=F32).astype(BF16)
    for k in range(groups):
        target = peer(k)
        first = jnp.int32(own - 1)
        for i in range(own - 2, -1, -1):
            first = jnp.where(owner_ref[ten * own + i] == target, i, first)
        second = jnp.int32(own - 1)
        for i in range(own - 2, 0, -1):
            hit = (owner_ref[ten * own + i] == target) & (i > first)
            second = jnp.where(hit, i, second)
        dst = unpacked if k == 0 else pack
        dst[k, 0] = comp[first]
        dst[k, 1] = comp[second]

    ends = jnp.where(z > 0, 1, 0) + jnp.where(z < chips - 1, 1, 0)
    pl.semaphore_wait(barrier, groups + ends)

    def pack_copy(k):
        return remote(pack.at[k], unpacked.at[k], pack_ss.at[k], pack_rs.at[k], tensor=peer(k))

    for k in range(1, groups):
        pack_copy(k).start()

    total = jnp.zeros((1, tokens), F32)
    for j in range(features // 128):
        part = x_ref[:, j * 128:(j + 1) * 128].astype(F32).T
        xhat[j * 128:(j + 1) * 128, :] = part
        total = total + jnp.sum(part * part, axis=0, keepdims=True)
    inv = lax.rsqrt(total / features + 1e-05)
    for j in range(features // 128):
        part = xhat[j * 128:(j + 1) * 128, :] * inv
        xhat[j * 128:(j + 1) * 128, :] = part
        normed[j * 128:(j + 1) * 128, :] = part.astype(BF16)

    def strip(ref, d):
        return ref[pl.ds(pl.multiple_of(d * rows, 16), rows), :]

    def grad_part(d):
        return jnp.dot(strip(normed, d), og_ref[...], preferred_element_type=F32)

    def sib_copy(c):
        return remote(sib_send.at[c], sib_recv.at[c], sib_ss.at[c], sib_rs.at[c], dp=sibling)

    def up_copy(c):
        return remote(up_send.at[c], up_recv.at[c], up_ss.at[c], up_rs.at[c], dp=dp + 2)

    def down_copy(c):
        return remote(down_send.at[c], down_recv.at[c], down_ss.at[c], down_rs.at[c], dp=dp - 2)

    order = []
    for k in range(chips):
        for c in (chips - 1 - k, k):
            if c not in order:
                order.append(c)
    for c in order:
        sib_send[c] = grad_part(2 * c + 1 - core).astype(BF16)
        sib_copy(c).start()

    def pair_sum(c):
        mine = grad_part(2 * c + core)
        sib_copy(c).wait_recv()
        return mine + sib_recv[c].astype(F32)

    def up_first(c):
        up_send[c] = pair_sum(c).astype(BF16)
        up_copy(c).start()

    def down_first(c):
        down_send[c] = pair_sum(c).astype(BF16)
        down_copy(c).start()

    @pl.when(z == 0)
    def _():
        for c in range(chips - 1, 1, -1):
            up_first(c)
            if c > 2:
                up_copy(c).wait_send()

    @pl.when(z == chips - 1)
    def _():
        for c in range(chips - 2):
            down_first(c)
            if c < chips - 3:
                down_copy(c).wait_send()

    def chain_up(up):
        mine = pair_sum(up)
        up_copy(up).wait_recv()
        up_send[up] = (mine + up_recv[up].astype(F32)).astype(BF16)
        up_copy(up).start()

    def chain_down(down):
        mine = pair_sum(down)
        down_copy(down).wait_recv()
        down_send[down] = (mine + down_recv[down].astype(F32)).astype(BF16)
        down_copy(down).start()

    @pl.when((z == 1) & (z < chips - 1))
    def _():
        chain_up(chips - 1)

    @pl.when((z == chips - 2) & (z > 0))
    def _():
        chain_down(0)

    def chain(k):
        up, down = chips - 1 - k, k

        @pl.when((z > (1 if k == 0 else 0)) & (z < up))
        def _():
            chain_up(up)

        @pl.when((z < chips - (2 if k == 0 else 1)) & (z > down))
        def _():
            chain_down(down)

    places = [jnp.int32(0) for _ in range(own)]
    count = jnp.int32(0)
    for h in range(groups):
        slot = jnp.int32(0)
        k = lax.rem(ten - h + groups, groups)
        for i in range(own):
            hit = owner_ref[h * own + i] == ten
            for r in range(own):
                places[r] = jnp.where(hit & (count == r), k * 2 + slot, places[r])
            step = jnp.where(hit, 1, 0)
            slot, count = slot + step, count + step
    for k in range(1, groups):
        pack_copy(k).wait_recv()
    for r in range(own):
        stripes[dp, :, r * 128:(r + 1) * 128] = unpacked[places[r] // 2, places[r] % 2]

    def gather_up(d):
        return remote(stripes.at[d], stripes.at[d], gup_ss.at[d], gather_rs.at[d], dp=dp + 2)

    def gather_down(d):
        return remote(stripes.at[d], stripes.at[d], gdown_ss.at[d], gather_rs.at[d], dp=dp - 2)

    def gather_sib(d):
        return remote(stripes.at[d], stripes.at[d], gsib_ss.at[d], gather_rs.at[d], dp=sibling)

    half = rows // 2

    def flip(bit):
        x, y = ten % 2, ten // 2
        return y * 2 + (1 - x) if bit == 1 else (1 - y) * 2 + x

    def rows_of(h):
        return pl.ds(h * half, half)

    def dn_copy(d, bit, h):
        j = d % per
        return remote(
            dn_send.at[d, rows_of(h)], dn_recv.at[bit - 1, j, rows_of(h)],
            dn_ss.at[d, h], dn_rs.at[bit - 1, j, h], tensor=flip(bit),
        )

    def relay_copy(d, bit):
        h = bit - 1
        return remote(
            dn_send.at[d, rows_of(h)], relay.at[d], dn_ss.at[d, h], relay_rs.at[d],
            tensor=flip(bit),
        )

    def is_near(d, bit):
        return d // per == flip(bit)

    def is_far(d):
        return (d // per != ten) & (d // per != flip(1)) & (d // per != flip(2))

    def use(d):
        part = lax.dot_general(
            stripes[d], og_ref[...], (((1,), (1,)), ((), ())), preferred_element_type=F32
        ).astype(BF16)
        dn_send[d] = part

        @pl.when(is_far(d))
        def _():
            relay_copy(d, 1).start()
            relay_copy(d, 2).start()

        for bit in (1, 2):
            @pl.when(is_near(d, bit))
            def _():
                dn_copy(d, bit, bit - 1).start()

        dot_send[...] += jnp.sum(
            (part.astype(F32) * strip(xhat, d)).reshape(rows // 8, 8, tokens), axis=0
        )
        acc[...] += lax.dot_general(
            strip(normed, d), stripes[d], (((0,), (0,)), ((), ())), preferred_element_type=F32
        )

    def pass_on(d):
        for bit in (1, 2):
            @pl.when(is_near(d, bit))
            def _():
                h = 2 - bit
                relay_copy(d, 3 - bit).wait_recv()
                mine = dn_send[d, rows_of(h)].astype(F32)
                dn_send[d, rows_of(h)] = (mine + relay[d].astype(F32)).astype(BF16)
                dn_copy(d, bit, h).start()

    def pass_on_pair(s):
        @pl.when(z - s >= 0)
        def _():
            pass_on(dp - 2 * s)
            pass_on((z - s) * 2 + 1 - core)

        if s > 0:
            @pl.when(z + s < chips)
            def _():
                pass_on(dp + 2 * s)
                pass_on((z + s) * 2 + 1 - core)

    acc[...] = jnp.zeros_like(acc)
    dot_send[...] = jnp.zeros_like(dot_send)

    @pl.when(z < chips - 1)
    def _():
        gather_up(dp).start()

    @pl.when(z > 0)
    def _():
        gather_down(dp).start()

    gather_sib(dp).start()
    use(dp)

    def from_sibling(chip):
        d = chip * 2 + 1 - core
        gather_sib(d).wait_recv()
        use(d)

    from_sibling(z)
    for s in range(1, chips):
        @pl.when(z - s >= 0)
        def _():
            d = dp - 2 * s
            gather_up(d).wait_recv()

            @pl.when(z < chips - 1)
            def _():
                gather_up(d).start()

            gather_sib(d).start()

        @pl.when(z + s < chips)
        def _():
            d = dp + 2 * s
            gather_down(d).wait_recv()

            @pl.when(z > 0)
            def _():
                gather_down(d).start()

            gather_sib(d).start()

        if s == 1:
            @pl.when(z == 0)
            def _():
                up_first(1)

            @pl.when(z == chips - 1)
            def _():
                down_first(chips - 2)

        pass_on_pair(s - 1)

        if s == chips - 1:
            for k in range(chips - 1):
                chain(k)

        @pl.when(z - s >= 0)
        def _():
            use(dp - 2 * s)
            from_sibling(z - s)

        @pl.when(z + s < chips)
        def _():
            use(dp + 2 * s)
            from_sibling(z + s)

    def dot_copy(k):
        return remote(dot_send, dot_recv.at[k], dot_ss.at[k], dot_rs.at[k], tensor=peer(k))

    for k in range(1, groups):
        dot_copy(k).start()
    pass_on_pair(chips - 1)
    proj_ref[...] = acc[...].astype(BF16)

    sib_total = grad_part(dp)
    sib_copy(z).wait_recv()
    wg_ref[...] = sib_total + sib_recv[z].astype(F32)

    @pl.when(z > 0)
    def _():
        up_copy(z).wait_recv()
        wg_ref[...] += up_recv[z].astype(F32)

    @pl.when(z < chips - 1)
    def _():
        down_copy(z).wait_recv()
        wg_ref[...] += down_recv[z].astype(F32)

    dot = dot_send[...]
    for k in range(1, groups):
        dot_copy(k).wait_recv()
        dot = dot + dot_recv[k]
    mean = jnp.sum(dot, axis=0, keepdims=True) / features
    for j in range(per):
        at = ten * per + j
        full = dn_send[at].astype(F32)
        for bit in (1, 2):
            for h in (0, 1):
                dn_copy(at, bit, h).wait_recv()
            full = full + dn_recv[bit - 1, j].astype(F32)
        acc_t = inv * (full - strip(xhat, at) * mean)
        xhat[pl.ds(pl.multiple_of(at * rows, 16), rows), :] = acc_t
    for j in range(share // 128):
        rows_j = pl.ds(pl.multiple_of(ten * share + j * 128, 128), 128)
        gin_ref[:, j * 128:(j + 1) * 128] = xhat[rows_j, :].T.astype(BF16)

    for k in range(1, groups):
        pack_copy(k).wait_send()
        dot_copy(k).wait_send()
    for c in range(chips):
        sib_copy(c).wait_send()

        @pl.when((c > z) & ((z > 0) | (c <= 2)))
        def _():
            up_copy(c).wait_send()

        @pl.when((c < z) & ((z < chips - 1) | (c >= chips - 3)))
        def _():
            down_copy(c).wait_send()

        d = 2 * c + core
        gather_sib(d).wait_send()

        @pl.when((c <= z) & (z < chips - 1))
        def _():
            gather_up(d).wait_send()

        @pl.when((c >= z) & (z > 0))
        def _():
            gather_down(d).wait_send()

    for d in range(ranks):
        @pl.when(d // per != ten)
        def _():
            for h in (0, 1):
                dn_copy(d, 1, h).wait_send()


def fused(groups, ranks, inputs, old_weight, keep_cols, owner, out_grad):
    tokens, features = inputs.shape
    rows, _ = old_weight.shape
    cols = out_grad.shape[1]
    own = cols // 128
    chips = ranks // 2
    per = ranks // groups
    stripe = (rows, cols)
    dma = pltpu.SemaphoreType.DMA
    vmem = pl.BlockSpec(memory_space=pltpu.VMEM)
    smem = pl.BlockSpec(memory_space=pltpu.SMEM)
    return pl.pallas_call(
        functools.partial(fused_kernel, groups, ranks),
        out_shape=(
            jax.ShapeDtypeStruct((tokens, cols), BF16),
            jax.ShapeDtypeStruct((tokens, features // groups), BF16),
            jax.ShapeDtypeStruct(stripe, F32),
        ),
        in_specs=[vmem, vmem, vmem, smem, vmem],
        out_specs=(vmem, vmem, vmem),
        scratch_shapes=[
            pltpu.VMEM((own, rows, 128), BF16),
            pltpu.VMEM((groups, 2, rows, 128), BF16),
            pltpu.VMEM((groups, 2, rows, 128), BF16),
            pltpu.VMEM((features, tokens), F32),
            pltpu.VMEM((features, tokens), BF16),
            pltpu.VMEM((ranks,) + stripe, BF16),
            pltpu.VMEM((tokens, cols), F32),
            pltpu.VMEM((ranks, rows, tokens), BF16),
            pltpu.VMEM((2, per, rows, tokens), BF16),
            pltpu.VMEM((ranks, rows // 2, tokens), BF16),
            pltpu.VMEM((8, tokens), F32),
            pltpu.VMEM((groups, 8, tokens), F32),
        ]
        + [pltpu.VMEM((chips,) + stripe, BF16)] * 6
        + [dma((groups,))] * 2
        + [dma((chips,))] * 6
        + [dma((ranks,))] * 4
        + [dma((ranks, 2)), dma((2, per, 2)), dma((ranks,))]
        + [dma((groups,))] * 2,
        compiler_params=pltpu.CompilerParams(
            collective_id=0, has_side_effects=True, vmem_limit_bytes=26 * 1024 * 1024
        ),
    )(inputs, old_weight, keep_cols.reshape(-1, 128), owner, out_grad)


def plain(inputs, old_weight, keep_cols, owner, out_grad):
    groups = lax.axis_size("tensor")
    myself = lax.axis_index("tensor")
    blocks = owner.shape[0]
    own_blocks = blocks // groups
    keep_table = keep_cols.reshape(blocks, 128)
    block_ids = jnp.arange(blocks, dtype=jnp.int32)
    earlier = block_ids[None, :] < block_ids[:, None]
    same_owner = owner[:, None] == owner[None, :]
    owner_rank = jnp.sum(same_owner & earlier, axis=1)
    ranks_here = jnp.arange(own_blocks, dtype=jnp.int32)
    mine_match = (owner[None, :] == myself) & (owner_rank[None, :] == ranks_here[:, None])
    mine_ids = jnp.sum(jnp.where(mine_match, block_ids[None, :], 0), axis=1)
    every_column = lax.all_gather(old_weight, "tensor", axis=1, tiled=True)
    new_stripe = jnp.take(every_column, keep_table[mine_ids].reshape(-1), axis=1)
    expanded_output = inputs.astype(jnp.float32)
    inverse_sigma = lax.rsqrt(
        jnp.mean(expanded_output * expanded_output, axis=1, keepdims=True) + 1e-05
    )
    centered_input = expanded_output * inverse_sigma
    normalized_rows = centered_input.astype(jnp.bfloat16)
    tokens, width = inputs.shape
    piece = lax.all_gather(new_stripe, "dp", axis=0, tiled=True)
    normed_cols = normalized_rows
    proj_sum = jnp.dot(normed_cols, piece, preferred_element_type=jnp.float32)
    partial_term = lax.dot_general(
        out_grad, piece, (((1,), (1,)), ((), ())), preferred_element_type=jnp.float32
    )
    back_sum = partial_term
    proj_sum, back_sum = (proj_sum, back_sum)
    projected = proj_sum.astype(jnp.bfloat16)
    share = width // groups
    reduced_total = lax.psum(back_sum.astype(jnp.bfloat16), "tensor").astype(jnp.float32)
    inner_product = jnp.mean(reduced_total * centered_input, axis=1, keepdims=True)
    complete_gradient = inverse_sigma * (reduced_total - centered_input * inner_product)
    gradient_input = lax.dynamic_slice_in_dim(complete_gradient, myself * share, share, 1).astype(
        jnp.bfloat16
    )
    normed_cols = normalized_rows
    weight_grad = lax.psum_scatter(
        lax.dot_general(
            normed_cols, out_grad, (((0,), (0,)), ((), ())), preferred_element_type=jnp.float32
        ),
        "dp",
        scatter_dimension=0,
        tiled=True,
    )
    return (projected, gradient_input, weight_grad)


def solution(mesh):
    groups, ranks = mesh.shape["tensor"], mesh.shape["dp"]
    placed = (P("dp", None), P("dp", "tensor"), P(), P(), P("dp", "tensor"))

    def local(inputs, old_weight, keep_cols, owner, out_grad):
        rows, share = old_weight.shape[0], inputs.shape[1] // groups
        fits = rows % 32 == 0 and share % 128 == 0 and groups == 4 and ranks % 4 == 0
        if fits:
            return fused(groups, ranks, inputs, old_weight, keep_cols, owner, out_grad)
        return plain(inputs, old_weight, keep_cols, owner, out_grad)

    return jax.shard_map(
        local,
        mesh=mesh,
        in_specs=placed,
        out_specs=(P("dp", "tensor"), P("dp", "tensor"), P("dp", "tensor")),
        check_vma=False,
    )
```
